128 devices in a mesh: pipe: 4 (over z_lo, core), expert: 32 (over z_hi, x, y).
Axes of the slice: x: 4, y: 4, z: 4 (z_hi: 2, z_lo: 2; z = z_hi * 2 + z_lo), core: 2. Of those that a mesh axis runs over, the one named last changes fastest.
Arguments:
- grad_out: bfloat16 [4, 2, 2048, 3584], P('pipe', None, 'expert'), may hold values from -6 to 6
- x_slots: bfloat16 [4, 2, 32, 32, 20, 3584], P('pipe', None, 'expert'), may hold values from -6 to 6
- expert_ids: int32 [4, 2, 2048, 2], P('pipe', None, 'expert'), may hold values from 0 to 7, all different within a row; in each aligned block of 64 rows (0 to 63, 64 to 127, ..., all dimensions but the last counted through in order) at most 20 rows name the same one
- route_weights: float32 [4, 2, 2048, 2], P('pipe', None, 'expert'), may hold values from 0.1 to 1
- w_gate_up: bfloat16 [4, 2, 3584, 8192], P('pipe', None, None, 'expert'), may hold values from -0.09375 to 0.09375
- w_down: bfloat16 [4, 8192, 3584], P('pipe', 'expert'), may hold values from -0.1875 to 0.1875
Outputs:
- grad_acts: bfloat16 [4, 2, 2048, 3584], P('pipe', None, 'expert')
- grad_gate_up: bfloat16 [4, 2, 3584, 8192], P('pipe', None, None, 'expert')
- grad_down: bfloat16 [4, 8192, 3584], P('pipe', 'expert')
The draws below stay inside these ranges and needn't reach their ends.
Inputs may be any that keep to these rules, and one draw needn't show every extreme that they name: `expert_ids`: each row names 2 different experts. In each block of 64 rows along the token dimension (one device's tokens of one micro-batch) no expert is named more than 20 times, and in every draw some block names some expert exactly 20 times.
All inputs are finite; a program needn't handle non-finite values.
Results may differ from the reference program's by a relative error of at most 0.01.
Values may be sent and summed in bfloat16 or wider, within the bound.
No kernel may reach another device: no remote copies, remote signals or barrier semaphores. Data moves between devices by JAX's collectives and lax.ppermute only.
A program may use at most 192 MiB of HBM per device.

```python
import math
import jax
import jax.numpy as jnp
import numpy as np
from jax import lax

D = 3584
F = 1024
EXPERTS = 8
TOPK = 2
TOK_DEV = 64
CAP = 20
SPLIT = 4
F_DEV = 256
EF = 8192
TOKENS = 2048
N_PIPE = 4
N_EXPERT = 32


def block_levels(rng, dims, shards, low, largest):
    factor_of, own = 1.0, jax.random.fold_in(rng, 6)
    for position, blocks in shards:
        steps = jnp.exp(jax.random.uniform(jax.random.fold_in(own, position), (blocks,), jnp.float32, low / len(shards), largest / len(shards)))
        factor_of = factor_of * jnp.repeat(steps, dims[position] // blocks).reshape([-1 if axis == position else 1 for axis in range(len(dims))])
    return factor_of


def shared_out(own_key, own, number, rows, number_of, top, limit, slope):
    order = jax.random.permutation(own_key, number_of)
    packed, common = load_shares(number_of, rows * top, limit, slope, True), load_shares(number_of, rows * top, limit, slope, False)
    places = jnp.arange(number_of)

    def named(lengths, offset_by):
        used = int((lengths > 0).sum())
        fixed = max(1, used // 4)
        shifted = fixed + (places - fixed + offset_by * (used - fixed)) % max(1, number_of - fixed)
        return jnp.zeros((number_of,), jnp.int32).at[order[jnp.where(places < fixed, places, shifted)]].set(jnp.asarray(lengths, jnp.int32))

    lengths = jnp.where(number % 4 == 0, named(packed, number // 4), named(common, number - number // 4 - 1))
    mixed = jax.random.permutation(jax.random.fold_in(own, 3), number_of)
    donor, receiver = mixed[0:number_of // 2 * 2:2], mixed[1:number_of // 2 * 2:2]
    margin = jnp.minimum(lengths[donor] - 1, limit - lengths[receiver]) // 2
    margin = jnp.where((donor == order[0]) | (receiver == order[0]) | (lengths[receiver] == 0), 0, jnp.maximum(margin, 0))
    shifted = jax.random.randint(jax.random.fold_in(own, 4), (number_of // 2,), 0, 1 << 20) % (margin + 1)
    lengths = lengths.at[donor].add(-shifted).at[receiver].add(shifted)
    items = jnp.searchsorted(jnp.cumsum(lengths), jnp.arange(rows * top), side="right").astype(jnp.int32)
    table = items.reshape(top, rows).T
    table = table[jax.random.permutation(jax.random.fold_in(own, 1), rows)]
    offset_by = jax.random.randint(jax.random.fold_in(own, 2), (rows, 1), 0, top)
    return jnp.take_along_axis(table, (jnp.arange(top)[None, :] + offset_by) % top, axis=1)


def load_shares(amount, total, most, slope, full):
    loads = [(1 << 20) // math.isqrt(standing ** slope) + 1 for standing in range(1, amount + 1)]
    largest = most if full else min(most, max(-(-total // amount), total * loads[0] // sum(loads)))
    least = 1 if total - largest >= amount - 1 else 0
    holding, rest = [largest] + [least] * (amount - 1), total - largest - least * (amount - 1)
    while rest > 0:
        free = [i for i in range(1, amount) if holding[i] < largest] or [i for i in range(1, amount) if holding[i] < most]
        whole, budget = sum([loads[i] for i in free]), rest
        for i in free:
            more = min(most - holding[i], max(1, budget * loads[i] // whole), rest)
            holding[i] = holding[i] + more
            rest = rest - more
    return np.array(holding)


def scatter_about(key, shape, scale, reach, split=(), kind=jnp.bfloat16):
    values = jax.random.normal(key, shape, jnp.float32) * scale
    if len(split) > 0:
        values = block_levels(key, shape, split, -0.22, 0.18) * values
    return jnp.clip(values, min=-reach, max=reach).astype(kind)


def setup_inputs(seed: int = 0) -> dict:
    arg_keys = jax.random.split(jax.random.key(seed), 7)
    grad_out = scatter_about(arg_keys[0], (N_PIPE, 2, TOKENS, D), 1.0, 6.0, ((0, 4), (2, 32)))
    x_slots = scatter_about(arg_keys[1], (N_PIPE, 2, N_EXPERT, N_EXPERT, CAP, D), 1.0, 6.0, ((0, 4), (2, 32)))
    expert_ids_keys = jax.random.split(jax.random.fold_in(arg_keys[2], 1), N_PIPE * 2 * TOKENS // TOK_DEV)
    expert_ids_turns = jax.random.permutation(jax.random.fold_in(arg_keys[2], 3), N_PIPE * 2 * TOKENS // TOK_DEV)
    expert_ids = jax.vmap(lambda own, number: shared_out(jax.random.fold_in(arg_keys[2], 2), own, number, TOK_DEV, EXPERTS, TOPK, CAP, 1))(expert_ids_keys, expert_ids_turns).reshape((N_PIPE, 2, TOKENS, TOPK))
    route_weights = jnp.clip(jnp.exp(math.log(1.0) - 2.3025851 * jax.random.uniform(arg_keys[3], (N_PIPE, 2, TOKENS, TOPK), jnp.float32) ** block_levels(arg_keys[3], (N_PIPE, 2, TOKENS, TOPK), ((0, 4), (2, 32)), -0.2, 0.2)), 0.1, 1.0)
    w_gate_up = scatter_about(arg_keys[4], (N_PIPE, 2, D, EF), D ** -0.5, 0.09375, ((0, 4), (3, 32)))
    w_down = scatter_about(arg_keys[5], (N_PIPE, EF, D), F ** -0.5, 0.1875, ((0, 4), (1, 32)))
    return dict(grad_out=grad_out, x_slots=x_slots, expert_ids=expert_ids, route_weights=route_weights, w_gate_up=w_gate_up, w_down=w_down)


def expert_pass(arrived, kept_inputs, gate_up, down_rows):
    width = arrived.shape[-1]
    grad_rows = arrived.reshape(-1, width)
    input_rows = kept_inputs.reshape(-1, width)
    gate_pre = jnp.dot(input_rows, gate_up[0], preferred_element_type=jnp.float32)
    up_pre = jnp.dot(input_rows, gate_up[1], preferred_element_type=jnp.float32)
    sigmoid_gate = jax.nn.sigmoid(gate_pre)
    activated = gate_pre * sigmoid_gate
    hidden = (activated * up_pre).astype(jnp.bfloat16)
    back_hidden = jnp.einsum("rd,fd->rf", grad_rows, down_rows, preferred_element_type=jnp.float32)
    back_gate = (back_hidden * up_pre * sigmoid_gate * (1.0 + gate_pre * (1.0 - sigmoid_gate))).astype(jnp.bfloat16)
    back_up = (back_hidden * activated).astype(jnp.bfloat16)
    part_rows = jnp.einsum("rf,df->rd", back_gate, gate_up[0], preferred_element_type=jnp.float32)
    part_rows = part_rows + jnp.einsum("rf,df->rd", back_up, gate_up[1], preferred_element_type=jnp.float32)
    part_rows = part_rows.astype(jnp.bfloat16).reshape(arrived.shape)
    grad_gate = jnp.einsum("rd,rf->df", input_rows, back_gate, preferred_element_type=jnp.float32).astype(jnp.bfloat16)
    grad_up = jnp.einsum("rd,rf->df", input_rows, back_up, preferred_element_type=jnp.float32).astype(jnp.bfloat16)
    grad_down_part = jnp.einsum("rf,rd->fd", hidden, grad_rows, preferred_element_type=jnp.float32).astype(jnp.bfloat16)
    return part_rows, grad_gate, grad_up, grad_down_part


def one_device(bundle):
    return expert_pass(bundle[0], bundle[1], bundle[2], bundle[3])


def reference(grad_out, x_slots, expert_ids, route_weights, w_gate_up, w_down):
    shares = {}
    acts_rows = []
    half_pipe = N_PIPE // 2
    for pipe_row in range(N_PIPE):
        micro_rows = []
        for micro in range(2):
            section = pipe_row if micro == 0 else pipe_row ^ half_pipe
            blocks = expert_ids[pipe_row, micro].reshape(N_EXPERT, TOK_DEV * TOPK)
            onehot = (blocks[:, :, None] == jnp.arange(EXPERTS, dtype=jnp.int32)[None, None, :]).astype(jnp.int32)
            running = jnp.cumsum(onehot, axis=1)
            slot = jnp.sum((running - 1) * onehot, axis=2).astype(jnp.int32)
            source = jnp.broadcast_to(jnp.arange(N_EXPERT, dtype=jnp.int32)[:, None], blocks.shape)
            weighted = route_weights[pipe_row, micro][:, :, None] * grad_out[pipe_row, micro][:, None, :].astype(jnp.float32)
            weighted = weighted.astype(jnp.bfloat16).reshape(N_EXPERT, TOK_DEV * TOPK, D)
            sent = jnp.zeros((EXPERTS, N_EXPERT, CAP, D), jnp.bfloat16).at[blocks, source, slot].set(weighted)
            sent_dev = jnp.repeat(sent, SPLIT, axis=0)
            gate_up_dev = w_gate_up[section].reshape(2, D, N_EXPERT, F_DEV).transpose(2, 0, 1, 3)
            down_dev = w_down[section].reshape(N_EXPERT, F_DEV, D)
            parts, grad_gate, grad_up, grad_down_part = lax.map(one_device, (sent_dev, x_slots[pipe_row, micro], gate_up_dev, down_dev))
            shares[(pipe_row, micro)] = (grad_gate, grad_up, grad_down_part)
            summed = parts.astype(jnp.float32).reshape(EXPERTS, SPLIT, N_EXPERT, CAP, D).sum(axis=1)
            gathered = summed[blocks, source, slot]
            micro_rows.append(gathered.reshape(TOKENS, TOPK, D).sum(axis=1).astype(jnp.bfloat16))
        acts_rows.append(jnp.stack(micro_rows))
    grad_acts = jnp.stack(acts_rows)
    gate_up_out = []
    down_out = []
    for section in range(N_PIPE):
        first = shares[(section, 0)]
        second = shares[(section ^ half_pipe, 1)]
        total_gate = (first[0].astype(jnp.float32) + second[0].astype(jnp.float32)).astype(jnp.bfloat16)
        total_up = (first[1].astype(jnp.float32) + second[1].astype(jnp.float32)).astype(jnp.bfloat16)
        total_down = (first[2].astype(jnp.float32) + second[2].astype(jnp.float32)).astype(jnp.bfloat16)
        stacked = jnp.stack([total_gate, total_up]).transpose(0, 2, 1, 3).reshape(2, D, EF)
        gate_up_out.append(stacked)
        down_out.append(total_down.reshape(EF, D))
    return grad_acts, jnp.stack(gate_up_out), jnp.stack(down_out)
```

```python
import functools

import jax
import jax.numpy as jnp
from jax import lax
from jax.experimental import pallas as pl
from jax.experimental.pallas import tpu as pltpu
from jax.sharding import PartitionSpec as P

CAP = 20
TOPK = 2
NX = 4
NY = 4
NZ = 2
PAIR = NX * NZ
HALF = NX * CAP
CHUNK = NZ * HALF
MESSAGE = NZ * CAP

bf16 = jnp.bfloat16
f32 = jnp.float32


def to_y(value, step):
    return lax.ppermute(
        value,
        "expert",
        [(e, e // NY * NY + (e + step) % NY) for e in range(PAIR * NY)],
    )


def to_x(value, step):
    def there(e):
        z, x, y = e // (NX * NY), e // NY % NX, e % NY
        return (z * NX + (x + step) % NX) * NY + y

    return lax.ppermute(value, "expert", [(e, there(e)) for e in range(PAIR * NY)])


def to_z(value):
    return lax.ppermute(
        value, "expert", [(e, e ^ (NX * NY)) for e in range(PAIR * NY)]
    )


def to_mirror(value, flip_z):
    count = PAIR * NY
    half = lax.axis_size("pipe") // 2
    flip = NX * NY if flip_z else 0
    pairs = [
        (p * count + e, (p ^ half) * count + (e ^ flip))
        for p in range(lax.axis_size("pipe"))
        for e in range(count)
    ]
    return lax.ppermute(value, ("pipe", "expert"), pairs)


def slot_rows(ids, place, z, x, along):
    slots = []
    tokens = ids[0].shape[along]
    wide = (PAIR, tokens) if along == 1 else (tokens, PAIR)
    expert = lax.broadcasted_iota(jnp.int32, wide, 1 - along)
    named = [expert == one for one in ids]
    both = (named[0] | named[1]).astype(f32).astype(bf16)
    first = lax.broadcasted_iota(jnp.int32, (tokens, tokens), 0)
    second = lax.broadcasted_iota(jnp.int32, (tokens, tokens), 1)
    if along == 1:
        earlier = jnp.dot(both, (first < second).astype(f32).astype(bf16), preferred_element_type=f32)
    else:
        earlier = jnp.dot((second < first).astype(f32).astype(bf16), both, preferred_element_type=f32)
    for one, mask in zip(ids, named):
        slot = jnp.sum(jnp.where(mask, earlier, 0.0), axis=1 - along, keepdims=True)
        dx = (one - x) & (NX - 1)
        dz = (one // NX) ^ z
        slots.append(dx * MESSAGE + dz * CAP + slot.astype(jnp.int32))
    return slots


def pack_kernel(place, ids_ref, weights_ref, grad_ref, *outs):
    z, x = place[0], place[1]
    ids = [ids_ref[0, 0:1, :], ids_ref[0, 1:2, :]]
    rows = slot_rows(ids, place, z, x, 1)
    grad = grad_ref[0, 0].astype(f32)
    tokens = grad.shape[0]
    row = lax.broadcasted_iota(jnp.int32, (PAIR * CAP, tokens), 0)
    packed = None
    for r in range(TOPK):
        weighted = (weights_ref[0, 0][:, r : r + 1] * grad).astype(bf16)
        table = (row == rows[r]).astype(f32).astype(bf16)
        term = jnp.dot(table, weighted, preferred_element_type=f32)
        packed = term if packed is None else packed + term
    for dx in range(NX):
        outs[dx][...] = packed[dx * MESSAGE : (dx + 1) * MESSAGE].astype(bf16)


def pack(place, ids_t, weights, grad, micro):
    tokens, width = grad.shape[2:]
    block = width // 2
    return pl.pallas_call(
        pack_kernel,
        grid_spec=pltpu.PrefetchScalarGridSpec(
            num_scalar_prefetch=1,
            grid=(width // block,),
            in_specs=[
                pl.BlockSpec((1, TOPK, tokens), lambda i, s: (micro, 0, 0)),
                pl.BlockSpec((1, 1, tokens, TOPK), lambda i, s: (0, micro, 0, 0)),
                pl.BlockSpec((1, 1, tokens, block), lambda i, s: (0, micro, 0, i)),
            ],
            out_specs=[pl.BlockSpec((MESSAGE, block), lambda i, s: (0, i))] * NX,
        ),
        out_shape=[jax.ShapeDtypeStruct((MESSAGE, width), bf16)] * NX,
        compiler_params=pltpu.CompilerParams(vmem_limit_bytes=32 << 20),
        cost_estimate=pl.CostEstimate(
            flops=4 * PAIR * CAP * tokens * width,
            bytes_accessed=2 * width * (tokens + PAIR * CAP),
            transcendentals=0,
        ),
        name="pack",
    )(place, ids_t, weights, grad)


def unpack_kernel(place, ids_ref, *refs):
    z, x = place[0], place[1]
    parts, out = refs[:NX], refs[-1]
    ids = [ids_ref[0, 0][:, 0:1], ids_ref[0, 0][:, 1:2]]
    rows = slot_rows(ids, place, z, x, 0)
    tokens = ids[0].shape[0]
    total = None
    for dx in range(NX):
        column = lax.broadcasted_iota(jnp.int32, (tokens, MESSAGE), 1) + dx * MESSAGE
        table = ((column == rows[0]) | (column == rows[1])).astype(f32).astype(bf16)
        term = jnp.dot(table, parts[dx][...], preferred_element_type=f32)
        total = term if total is None else total + term
    out[0, 0] = total.astype(bf16)


def unpack(place, ids, parts, micro, before):
    tokens, width = ids.shape[2], parts[0].shape[1]
    block = width // 2
    in_specs = [pl.BlockSpec((1, 1, tokens, TOPK), lambda i, s: (0, micro, 0, 0))]
    in_specs += [pl.BlockSpec((MESSAGE, block), lambda i, s: (0, i))] * NX
    operands = [place, ids, *parts]
    aliases = {}
    if before is not None:
        in_specs.append(pl.BlockSpec(memory_space=pl.ANY))
        operands.append(before)
        aliases = {len(operands) - 1: 0}
    return pl.pallas_call(
        unpack_kernel,
        grid_spec=pltpu.PrefetchScalarGridSpec(
            num_scalar_prefetch=1,
            grid=(width // block,),
            in_specs=in_specs,
            out_specs=pl.BlockSpec((1, 1, tokens, block), lambda i, s: (0, micro, 0, i)),
        ),
        out_shape=jax.ShapeDtypeStruct((1, 2, tokens, width), bf16),
        input_output_aliases=aliases,
        compiler_params=pltpu.CompilerParams(vmem_limit_bytes=32 << 20),
        cost_estimate=pl.CostEstimate(
            flops=2 * PAIR * CAP * tokens * width,
            bytes_accessed=2 * width * (tokens + PAIR * CAP),
            transcendentals=0,
        ),
        name="unpack",
    )(*operands)


def order_kernel(place, *refs):
    out = refs[-1]
    for i, ref in enumerate(refs[:-1]):
        out[i * CAP : (i + 1) * CAP, :] = ref[0, 0, 0, 0]


def order_inputs(place, x_slots, micro, dy):
    width = x_slots.shape[-1]
    block = width // 2

    def spec(dz, dx):
        def index(i, s):
            source = ((s[0] ^ dz) * NX + ((s[1] - dx) & (NX - 1))) * NY + (
                (s[2] - dy) & (NY - 1)
            )
            return (0, micro, 0, source, 0, i)

        return pl.BlockSpec((1, 1, 1, 1, CAP, block), index)

    return pl.pallas_call(
        order_kernel,
        grid_spec=pltpu.PrefetchScalarGridSpec(
            num_scalar_prefetch=1,
            grid=(width // block,),
            in_specs=[spec(dz, dx) for dz in range(NZ) for dx in range(NX)],
            out_specs=pl.BlockSpec((CHUNK, block), lambda i, s: (0, i)),
        ),
        out_shape=jax.ShapeDtypeStruct((CHUNK, width), bf16),
        compiler_params=pltpu.CompilerParams(vmem_limit_bytes=32 << 20),
        cost_estimate=pl.CostEstimate(
            flops=0, bytes_accessed=4 * width * CHUNK, transcendentals=0
        ),
        name="order",
    )(place, *[x_slots] * PAIR)


def across(a, b):
    return lax.dot_general(a, b, (((1,), (1,)), ((), ())), preferred_element_type=f32)


def part_kernel(x_ref, ya_ref, yb_ref, w_ref, d_ref, pa_ref, pb_ref, h_ref):
    x = x_ref[...]
    gate = jnp.dot(x, w_ref[0, 0], preferred_element_type=f32)
    up = jnp.dot(x, w_ref[0, 1], preferred_element_type=f32)
    y = jnp.concatenate([ya_ref[...], yb_ref[...]], axis=0)
    back = across(y, d_ref[0])
    sigmoid = jax.nn.sigmoid(gate)
    activated = gate * sigmoid
    back_gate = (back * up * sigmoid * (1.0 + gate * (1.0 - sigmoid))).astype(bf16)
    back_up = (back * activated).astype(bf16)
    units = gate.shape[1]
    h_ref[:, 0:units] = back_gate
    h_ref[:, units : 2 * units] = back_up
    h_ref[:, 2 * units : 3 * units] = (activated * up).astype(bf16)
    part = across(back_gate, w_ref[0, 0]) + across(back_up, w_ref[0, 1])
    pa_ref[...] = part[:HALF].astype(bf16)
    pb_ref[...] = part[HALF:].astype(bf16)


def part_pass(x, ya, yb, w_gate_up, w_down):
    width = x.shape[1]
    units = w_down.shape[1]
    half = jax.ShapeDtypeStruct((HALF, width), bf16)
    return pl.pallas_call(
        part_kernel,
        out_shape=[half, half, jax.ShapeDtypeStruct((CHUNK, 3 * units), bf16)],
        compiler_params=pltpu.CompilerParams(vmem_limit_bytes=32 << 20),
        cost_estimate=pl.CostEstimate(
            flops=10 * CHUNK * width * units,
            bytes_accessed=2 * width * (3 * CHUNK + 3 * units),
            transcendentals=CHUNK * units,
        ),
        name="part",
    )(x, ya, yb, w_gate_up, w_down)


def share_kernel(count, *refs):
    xs, ys, hs = refs[:count], refs[count : 3 * count], refs[3 * count : 4 * count]
    gate_up_ref, down_ref = refs[4 * count :]
    units = down_ref.shape[1]
    x = jnp.concatenate([r[...] for r in xs], axis=0)
    y = jnp.concatenate([r[...] for r in ys], axis=0)
    h = jnp.concatenate([r[...] for r in hs], axis=0)

    def over_rows(a, b):
        return lax.dot_general(a, b, (((0,), (0,)), ((), ())), preferred_element_type=f32)

    gate_up = over_rows(x, h[:, : 2 * units])
    gate_up_ref[0, 0] = gate_up[:, :units].astype(bf16)
    gate_up_ref[0, 1] = gate_up[:, units:].astype(bf16)
    down_ref[0] = over_rows(h[:, 2 * units :], y).astype(bf16)


def shares(xs, ys, hs):
    width = xs[0].shape[1]
    units = hs[0].shape[1] // 3
    count = len(xs)
    block = 512 if width % 512 == 0 else 256
    by_column = [pl.BlockSpec((CHUNK, block), lambda i: (0, i))] * count
    by_column += [pl.BlockSpec((HALF, block), lambda i: (0, i))] * (2 * count)
    whole = [pl.BlockSpec((CHUNK, 3 * units), lambda i: (0, 0))] * count
    return pl.pallas_call(
        functools.partial(share_kernel, count),
        grid=(width // block,),
        in_specs=by_column + whole,
        out_specs=[
            pl.BlockSpec((1, 2, block, units), lambda i: (0, 0, i, 0)),
            pl.BlockSpec((1, units, block), lambda i: (0, 0, i)),
        ],
        out_shape=[
            jax.ShapeDtypeStruct((1, 2, width, units), bf16),
            jax.ShapeDtypeStruct((1, units, width), bf16),
        ],
        compiler_params=pltpu.CompilerParams(vmem_limit_bytes=48 << 20),
        cost_estimate=pl.CostEstimate(
            flops=6 * count * CHUNK * width * units,
            bytes_accessed=4 * width * count * CHUNK + 6 * width * units,
            transcendentals=0,
        ),
        name="shares",
    )(*xs, *ys, *hs)


def add(*terms):
    total = terms[0].astype(f32)
    for term in terms[1:]:
        total = total + term.astype(f32)
    return total.astype(bf16)


def send_slots(blocks, micro):
    blocks = [blocks[0]] + [to_x(blocks[dx], dx) for dx in range(1, NX)]
    near = jnp.concatenate([b[:CAP] for b in blocks], axis=0)
    far = jnp.concatenate([b[CAP:] for b in blocks], axis=0)
    if micro == 0:
        a, b = near, to_z(far)
    else:
        a, b = to_mirror(near, False), to_mirror(far, True)
    up_a, down_a = to_y(a, 1), to_y(a, -1)
    up_b, down_b = to_y(b, 1), to_y(b, -1)
    twice_a, twice_b = to_y(up_a, 1), to_y(down_b, -1)
    return [(a, b), (up_a, up_b), (twice_a, twice_b), (down_a, down_b)]


def return_parts(parts, micro):
    from_up = to_y(parts[2][0], -1)
    from_down = to_y(parts[2][1], 1)
    b1 = to_y(parts[1][1], -1)
    a3 = to_y(parts[3][0], 1)
    a1 = to_y(add(parts[1][0], from_up), -1)
    b3 = to_y(add(parts[3][1], from_down), 1)
    b = add(parts[0][1], b1, b3)
    a = add(parts[0][0], a1, a3)
    if micro == 0:
        near, far = a, to_z(b)
    else:
        near, far = to_mirror(a, False), to_mirror(b, True)
    messages = []
    for dx in range(NX):
        rows = slice(dx * CAP, (dx + 1) * CAP)
        message = jnp.concatenate([near[rows], far[rows]], axis=0)
        messages.append(to_x(message, -dx) if dx else message)
    return messages


def on_device(grad_out, x_slots, expert_ids, route_weights, w_gate_up, w_down):
    e = lax.axis_index("expert")
    place = jnp.stack([e // (NX * NY), e // NY % NX, e % NY]).astype(jnp.int32)
    ids_t = jnp.swapaxes(expert_ids[0], 1, 2)
    order = (2, 1, 3, 0)

    blocks = [pack(place, ids_t, route_weights, grad_out, k) for k in range(2)]
    inputs = [{}, {}]
    for dy in order:
        inputs[1][dy] = to_mirror(order_inputs(place, x_slots, 1, dy), False)
    for dy in order:
        inputs[0][dy] = order_inputs(place, x_slots, 0, dy)

    slots = [send_slots(blocks[k], k) for k in range(2)]
    results, hidden = [], []
    for k in range(2):
        parts, kept = {}, {}
        for dy in order:
            a, b, kept[dy] = part_pass(inputs[k][dy], *slots[k][dy], w_gate_up, w_down)
            parts[dy] = (a, b)
        hidden.append(kept)
        results.append(return_parts(parts, k))

    acts = unpack(place, expert_ids, results[0], 0, None)
    acts = unpack(place, expert_ids, results[1], 1, acts)
    every = [(k, dy) for k in range(2) for dy in range(NY)]
    gate_up, down = shares(
        [inputs[k][dy] for k, dy in every],
        [half for k, dy in every for half in slots[k][dy]],
        [hidden[k][dy] for k, dy in every],
    )
    return acts, gate_up, down


def solution(mesh):
    return jax.shard_map(
        on_device,
        mesh=mesh,
        in_specs=(
            P("pipe", None, "expert", None),
            P("pipe", None, "expert", None, None, None),
            P("pipe", None, "expert", None),
            P("pipe", None, "expert", None),
            P("pipe", None, None, "expert"),
            P("pipe", "expert", None),
        ),
        out_specs=(
            P("pipe", None, "expert", None),
            P("pipe", None, None, "expert"),
            P("pipe", "expert", None),
        ),
        check_vma=False,
    )
```

```python
import functools

import jax
import jax.numpy as jnp
from jax import lax
from jax.experimental import pallas as pl
from jax.experimental.pallas import tpu as pltpu
from jax.sharding import PartitionSpec as P

CAP = 20
TOPK = 2
NX = 4
NY = 4
NZ = 2
PAIR = NX * NZ
HALF = NX * CAP
CHUNK = NZ * HALF
MESSAGE = NZ * CAP

SIZES = (192, 256, 192)
DEPTH = 2


bf16 = jnp.bfloat16
f32 = jnp.float32
LIGHT = pl.CostEstimate(flops=1, bytes_accessed=1, transcendentals=0)


def to_y(value, step):
    return lax.ppermute(
        value,
        "expert",
        [(e, e // NY * NY + (e + step) % NY) for e in range(PAIR * NY)],
    )


def to_x(value, step):
    def there(e):
        z, x, y = e // (NX * NY), e // NY % NX, e % NY
        return (z * NX + (x + step) % NX) * NY + y

    return lax.ppermute(value, "expert", [(e, there(e)) for e in range(PAIR * NY)])


def to_z(value):
    return lax.ppermute(
        value, "expert", [(e, e ^ (NX * NY)) for e in range(PAIR * NY)]
    )


def to_mirror(value, flip_z):
    count = PAIR * NY
    half = lax.axis_size("pipe") // 2
    flip = NX * NY if flip_z else 0
    pairs = [
        (p * count + e, (p ^ half) * count + (e ^ flip))
        for p in range(lax.axis_size("pipe"))
        for e in range(count)
    ]
    return lax.ppermute(value, ("pipe", "expert"), pairs)


def after(value, *others):
    return lax.optimization_barrier((value, others))[0]


def to_column(row):
    n = row.shape[1]
    first = lax.broadcasted_iota(jnp.int32, (n, n), 0)
    second = lax.broadcasted_iota(jnp.int32, (n, n), 1)
    return jnp.sum(jnp.where(first == second, row, jnp.zeros_like(row)), axis=1, keepdims=True)


def slot_rows(ids, z, x, along):
    slots = []
    tokens = ids[0].shape[along]
    wide = (PAIR, tokens) if along == 1 else (tokens, PAIR)
    expert = lax.broadcasted_iota(jnp.int32, wide, 1 - along)
    named = [expert == one for one in ids]
    both = (named[0] | named[1]).astype(f32).astype(bf16)
    first = lax.broadcasted_iota(jnp.int32, (tokens, tokens), 0)
    second = lax.broadcasted_iota(jnp.int32, (tokens, tokens), 1)
    if along == 1:
        earlier = jnp.dot(both, (first < second).astype(f32).astype(bf16), preferred_element_type=f32)
    else:
        earlier = jnp.dot((second < first).astype(f32).astype(bf16), both, preferred_element_type=f32)
    for one, mask in zip(ids, named):
        slot = jnp.sum(jnp.where(mask, earlier, 0.0), axis=1 - along, keepdims=True)
        dx = (one - x) & (NX - 1)
        dz = (one // NX) ^ z
        slots.append(dx * MESSAGE + dz * CAP + slot.astype(jnp.int32))
    return slots


def pack_kernel(place, ids_ref, weights_ref, grad_ref, *outs):
    z, x = place[0], place[1]
    for k in range(2):
        ids = [ids_ref[k, r : r + 1, :] for r in range(TOPK)]
        rows = slot_rows(ids, z, x, 1)
        grad = grad_ref[0, k].astype(f32)
        row = lax.broadcasted_iota(jnp.int32, (PAIR * CAP, grad.shape[0]), 0)
        packed = None
        for r in range(TOPK):
            weighted = (to_column(weights_ref[k, r : r + 1, :]) * grad).astype(bf16)
            table = (row == rows[r]).astype(f32).astype(bf16)
            term = jnp.dot(table, weighted, preferred_element_type=f32)
            packed = term if packed is None else packed + term
        for dx in range(NX):
            piece = packed[dx * MESSAGE : (dx + 1) * MESSAGE].astype(bf16)
            outs[dx][k * MESSAGE : (k + 1) * MESSAGE, :] = piece


def pack(place, ids_t, weights_t, grad):
    tokens, width = grad.shape[2:]
    block = width // 2
    return pl.pallas_call(
        pack_kernel,
        grid_spec=pltpu.PrefetchScalarGridSpec(
            num_scalar_prefetch=1,
            grid=(width // block,),
            in_specs=[
                pl.BlockSpec((2, TOPK, tokens), lambda i, s: (0, 0, 0)),
                pl.BlockSpec((2, TOPK, tokens), lambda i, s: (0, 0, 0)),
                pl.BlockSpec((1, 2, tokens, block), lambda i, s: (0, 0, 0, i)),
            ],
            out_specs=[pl.BlockSpec((2 * MESSAGE, block), lambda i, s: (0, i))] * NX,
        ),
        out_shape=[jax.ShapeDtypeStruct((2 * MESSAGE, width), bf16)] * NX,
        compiler_params=pltpu.CompilerParams(vmem_limit_bytes=32 << 20),
        cost_estimate=LIGHT,
        name="pack",
    )(place, ids_t, weights_t, grad)


def unpack_kernel(place, ids_ref, *refs):
    z, x = place[0], place[1]
    parts, out = refs[:NX], refs[-1]
    ids = [to_column(ids_ref[0, r : r + 1, :].astype(f32)).astype(jnp.int32) for r in range(TOPK)]
    rows = slot_rows(ids, z, x, 0)
    tokens = ids[0].shape[0]
    total = None
    for dx in range(NX):
        column = lax.broadcasted_iota(jnp.int32, (tokens, MESSAGE), 1) + dx * MESSAGE
        table = ((column == rows[0]) | (column == rows[1])).astype(f32).astype(bf16)
        term = jnp.dot(table, parts[dx][...], preferred_element_type=f32)
        total = term if total is None else total + term
    out[0, 0] = total.astype(bf16)


def unpack(place, ids_t, parts, micro, first, width, before):
    tokens, block = ids_t.shape[2], parts[0].shape[1]
    in_specs = [pl.BlockSpec((1, TOPK, tokens), lambda i, s: (micro, 0, 0))]
    in_specs += [pl.BlockSpec((MESSAGE, block), lambda i, s: (0, 0))] * NX
    operands = [place, ids_t, *parts]
    aliases = {}
    if before is not None:
        in_specs.append(pl.BlockSpec(memory_space=pl.ANY))
        operands.append(before)
        aliases = {len(operands) - 1: 0}
    return pl.pallas_call(
        unpack_kernel,
        grid_spec=pltpu.PrefetchScalarGridSpec(
            num_scalar_prefetch=1,
            grid=(1,),
            in_specs=in_specs,
            out_specs=pl.BlockSpec((1, 1, tokens, block), lambda i, s: (0, micro, 0, first)),
        ),
        out_shape=jax.ShapeDtypeStruct((1, 2, tokens, width), bf16),
        input_output_aliases=aliases,
        compiler_params=pltpu.CompilerParams(vmem_limit_bytes=32 << 20),
        cost_estimate=LIGHT,
        name="unpack",
    )(*operands)


def kept_row(place, row):
    half = sum((row >= k * HALF).astype(jnp.int32) for k in range(1, NY * NZ))
    left = row - half * HALF
    dx = sum((left >= k * CAP).astype(jnp.int32) for k in range(1, NX))
    slot = left - dx * CAP
    dy, dz = half // NZ, half & (NZ - 1)
    source = ((place[0] ^ dz) * NX + ((place[1] - dx) & (NX - 1))) * NY
    source = source + ((place[2] - dy) & (NY - 1))
    return slot * (PAIR * NY) + source


def ahead_kernel(x_ref, w_ref, out):
    x = x_ref[...]
    units = w_ref.shape[3]
    for i in range(2):
        kept = jnp.dot(x, w_ref[0, i], preferred_element_type=f32)
        high = kept.astype(bf16)
        out[:, 2 * i * units : (2 * i + 1) * units] = high
        out[:, (2 * i + 1) * units : (2 * i + 2) * units] = (kept - high.astype(f32)).astype(bf16)


def ahead(piece, count, w_gate_up):
    width, units = w_gate_up.shape[2:]
    return pl.pallas_call(
        ahead_kernel,
        grid=(1,),
        in_specs=[
            pl.BlockSpec((count, width), lambda i: (0, 0)),
            pl.BlockSpec((1, 2, width, units), lambda i: (0, 0, 0, 0)),
        ],
        out_specs=pl.BlockSpec((count, 4 * units), lambda i: (0, 0)),
        out_shape=jax.ShapeDtypeStruct((count, 4 * units), bf16),
        compiler_params=pltpu.CompilerParams(vmem_limit_bytes=32 << 20),
        cost_estimate=LIGHT,
        name="ahead",
    )(piece, w_gate_up)


def across(a, b):
    return lax.dot_general(a, b, (((1,), (1,)), ((), ())), preferred_element_type=f32)


def part_kernel(pieces, dy, place, *refs):
    gs, refs = refs[:pieces], refs[pieces:]
    ya_ref, yb_ref, w_ref, d_ref, *outs = refs
    h_ref = outs[-1]
    units = d_ref.shape[1]
    wanted = kept_row(place, lax.broadcasted_iota(jnp.int32, (CHUNK, 1), 0) + dy * CHUNK)
    column = lax.broadcasted_iota(jnp.int32, (CHUNK, NY * CHUNK), 1)
    table = (column == wanted).astype(f32).astype(bf16)
    kept = jnp.concatenate([ref[...] for ref in gs], axis=0)
    kept = jnp.dot(table, kept, preferred_element_type=f32)
    gate = kept[:, :units] + kept[:, units : 2 * units]
    up = kept[:, 2 * units : 3 * units] + kept[:, 3 * units :]
    y = jnp.concatenate([ya_ref[...], yb_ref[...]], axis=0)
    back = across(y, d_ref[0])
    sigmoid = jax.nn.sigmoid(gate)
    activated = gate * sigmoid
    back_gate = (back * up * sigmoid * (1.0 + gate * (1.0 - sigmoid))).astype(bf16)
    back_up = (back * activated).astype(bf16)
    h_ref[:, 0:units] = back_gate
    h_ref[:, units : 2 * units] = back_up
    h_ref[:, 2 * units : 3 * units] = (activated * up).astype(bf16)
    part = across(back_gate, w_ref[0, 0]) + across(back_up, w_ref[0, 1])
    cuts = len(outs) // NZ
    block = part.shape[1] // cuts
    for dz in range(NZ):
        for cut in range(cuts):
            piece = part[dz * HALF : (dz + 1) * HALF, cut * block : (cut + 1) * block]
            outs[cut * NZ + dz][...] = piece.astype(bf16)


def part_pass(place, gates, dy, ya, yb, w_gate_up, w_down, cuts):
    width = ya.shape[1]
    units = w_down.shape[1]
    cut = pl.BlockSpec((HALF, width // cuts), lambda i, s: (0, 0))
    return pl.pallas_call(
        functools.partial(part_kernel, len(gates), dy),
        grid_spec=pltpu.PrefetchScalarGridSpec(
            num_scalar_prefetch=1,
            grid=(1,),
            in_specs=[pl.BlockSpec(g.shape, lambda i, s: (0, 0)) for g in gates]
            + [
                pl.BlockSpec((HALF, width), lambda i, s: (0, 0)),
                pl.BlockSpec((HALF, width), lambda i, s: (0, 0)),
                pl.BlockSpec((1, 2, width, units), lambda i, s: (0, 0, 0, 0)),
                pl.BlockSpec((1, units, width), lambda i, s: (0, 0, 0)),
            ],
            out_specs=[cut] * (NZ * cuts) + [pl.BlockSpec((CHUNK, 3 * units), lambda i, s: (0, 0))],
        ),
        out_shape=[jax.ShapeDtypeStruct((HALF, width // cuts), bf16)] * (NZ * cuts)
        + [jax.ShapeDtypeStruct((CHUNK, 3 * units), bf16)],
        compiler_params=pltpu.CompilerParams(vmem_limit_bytes=32 << 20),
        cost_estimate=LIGHT,
        name="part",
    )(place, *gates, ya, yb, w_gate_up, w_down)


def share_kernel(pieces, more, place, *refs):
    xs, refs = refs[:pieces], refs[pieces:]
    ys, hs, refs = refs[: NZ * NY], refs[NZ * NY : NZ * NY + NY], refs[NZ * NY + NY :]
    before, refs = refs[:more], refs[more:]
    gate_up_ref, down_ref, moved, hidden = refs
    units = down_ref.shape[1]
    rows = NY * CHUNK

    @pl.when(pl.program_id(0) == 0)
    def _():
        wanted = kept_row(place, lax.broadcasted_iota(jnp.int32, (1, rows), 1))
        row = lax.broadcasted_iota(jnp.int32, (rows, rows), 0)
        table = (row == wanted).astype(f32).astype(bf16)
        h = jnp.concatenate([r[...] for r in hs], axis=0)
        kept = jnp.dot(table, h[:, : 2 * units], preferred_element_type=f32)
        moved[...] = kept.astype(bf16)
        hidden[...] = h[:, 2 * units :]

    x = jnp.concatenate([r[...] for r in xs], axis=0)
    y = jnp.concatenate([r[...] for r in ys], axis=0)

    def over_rows(a, b):
        return lax.dot_general(a, b, (((0,), (0,)), ((), ())), preferred_element_type=f32)

    gate_up = over_rows(x, moved[...])
    share = [gate_up[:, :units], gate_up[:, units:], over_rows(hidden[...], y)]
    if before:
        share[0] = share[0] + before[0][0, 0].astype(f32)
        share[1] = share[1] + before[0][0, 1].astype(f32)
        share[2] = share[2] + before[1][0].astype(f32)
    gate_up_ref[0, 0] = share[0].astype(bf16)
    gate_up_ref[0, 1] = share[1].astype(bf16)
    down_ref[0] = share[2].astype(bf16)


def shares(place, xs, sizes, ys, hs, before):
    width = ys[0].shape[1]
    units = hs[0].shape[1] // 3
    block = 512 if width % 512 == 0 else 256
    by_column = [pl.BlockSpec((size, block), lambda i, s: (0, i)) for size in sizes]
    by_column += [pl.BlockSpec((HALF, block), lambda i, s: (0, i))] * (NZ * NY)
    whole = [pl.BlockSpec((CHUNK, 3 * units), lambda i, s: (0, 0))] * NY
    outs = [
        pl.BlockSpec((1, 2, block, units), lambda i, s: (0, 0, i, 0)),
        pl.BlockSpec((1, units, block), lambda i, s: (0, 0, i)),
    ]
    return pl.pallas_call(
        functools.partial(share_kernel, len(xs), len(before)),
        grid_spec=pltpu.PrefetchScalarGridSpec(
            num_scalar_prefetch=1,
            grid=(width // block,),
            in_specs=by_column + whole + outs[: len(before)],
            out_specs=outs,
            scratch_shapes=[
                pltpu.VMEM((NY * CHUNK, 2 * units), bf16),
                pltpu.VMEM((NY * CHUNK, units), bf16),
            ],
        ),
        out_shape=[
            jax.ShapeDtypeStruct((1, 2, width, units), bf16),
            jax.ShapeDtypeStruct((1, units, width), bf16),
        ],
        compiler_params=pltpu.CompilerParams(vmem_limit_bytes=32 << 20),
        cost_estimate=LIGHT,
        name="shares",
    )(place, *xs, *ys, *hs, *before)


def add(*terms):
    total = terms[0].astype(f32)
    for term in terms[1:]:
        total = total + term.astype(f32)
    return total.astype(bf16)


def over_x(blocks):
    return [blocks[0]] + [to_x(blocks[dx], dx) for dx in range(1, NX)]


def over_z(messages, micro):
    at = micro * MESSAGE
    near = jnp.concatenate([m[at : at + CAP] for m in messages], axis=0)
    far = jnp.concatenate([m[at + CAP : at + MESSAGE] for m in messages], axis=0)
    if micro == 0:
        return near, to_z(far)
    return to_mirror(near, False), to_mirror(far, True)


class Ring:
    def __init__(self):
        self.done = {1: [], -1: []}

    def send(self, value, step, *events):
        before = len(self.done[step]) - DEPTH
        if before >= 0:
            events += tuple(done[before] for done in self.done.values() if len(done) > before)
        self.done[step].append(to_y(after(value, *events) if events else value, step))
        return self.done[step][-1]


def home_z(a, b, micro):
    if micro == 0:
        return a, to_z(b)
    return to_mirror(a, False), to_mirror(b, True)


def home_x(near, far):
    messages = []
    for dx in range(NX):
        rows = slice(dx * CAP, (dx + 1) * CAP)
        message = jnp.concatenate([near[rows], far[rows]], axis=0)
        messages.append(to_x(message, -dx) if dx else message)
    return messages


def on_device(grad_out, x_slots, expert_ids, route_weights, w_gate_up, w_down):
    e = lax.axis_index("expert")
    width = grad_out.shape[-1]
    place = jnp.stack([e // (NX * NY), e // NY % NX, e % NY]).astype(jnp.int32)
    ids_t = jnp.swapaxes(expert_ids[0], 1, 2)
    weights_t = jnp.swapaxes(route_weights[0], 1, 2)
    rows = jnp.swapaxes(x_slots, 3, 4).reshape(-1, width)
    every = NY * CHUNK
    order = (2, 1, 3, 0)
    starts = [every + sum(SIZES[:i]) for i in range(len(SIZES))]
    moved = []

    def move(*events):
        at, size = starts[len(moved)], SIZES[len(moved)]
        value = rows[at : at + size]
        moved.append(to_mirror(after(value, *events) if events else value, False))

    ring = Ring()

    messages = over_x(pack(place, ids_t, weights_t, grad_out))
    gates = ahead(rows, every, w_gate_up)
    move()
    messages = after(messages, gates, moved[0])
    a, b = over_z(messages, 0)
    near_far = over_z(messages, 1)
    up_a, down_a = ring.send(a, 1), ring.send(a, -1)
    b = after(b, up_a, down_a)
    up_b, down_b = ring.send(b, 1), ring.send(b, -1)
    twice_a, twice_b = ring.send(up_a, 1, *near_far), ring.send(down_b, -1, *near_far)
    slots = [[(a, b), (up_a, up_b), (twice_a, twice_b), (down_a, down_b)]]
    move(near_far, moved[0])
    a, b = near_far
    up_a, down_a = ring.send(a, 1), ring.send(a, -1)
    up_b, down_b = ring.send(b, 1), ring.send(b, -1)
    hidden = [{}, {}]

    def compute(k, gates):
        parts = [None] * NY
        for dy in order:
            *parts[dy], hidden[k][dy] = part_pass(
                place, gates, dy, *slots[k][dy], w_gate_up, w_down, 1
            )
        return parts

    def sum_up(parts, *between):
        met = ring.send(parts[2][1], 1), ring.send(parts[2][0], -1)
        b1 = ring.send(parts[1][1], -1)
        a3 = ring.send(parts[3][0], 1)
        a1 = ring.send(add(parts[1][0], met[1]), -1, *between)
        b3 = ring.send(add(parts[3][1], met[0]), 1, *between)
        return met, (parts[0][0], a1, a3), (parts[0][1], b1, b3)

    twice_a, twice_b = ring.send(up_a, 1, moved[1]), ring.send(down_b, -1, moved[1])
    slots.append([(a, b), (up_a, up_b), (twice_a, twice_b), (down_a, down_b)])
    move(moved[1])
    parts = compute(0, [gates])
    met, sums_a, sums_b = sum_up(parts, moved[2])
    back = home_z(add(*sums_a), add(*sums_b), 0)
    messages = home_x(*back)
    acts = unpack(place, ids_t, messages, 0, 0, width, None)
    grads = shares(
        place,
        [rows],
        [every],
        [half for dy in range(NY) for half in slots[0][dy]],
        after([hidden[0][dy] for dy in range(NY)], met),
        [],
    )

    *early, last = moved
    gates = [ahead(piece, size, w_gate_up) for piece, size in zip(early, SIZES)]
    gates.append(ahead(after(last, met, gates, grads), SIZES[-1], w_gate_up))
    parts = compute(1, gates)
    met, sums_a, sums_b = sum_up(parts, *back)
    gate_up, down = shares(
        place,
        moved,
        SIZES,
        [half for dy in range(NY) for half in slots[1][dy]],
        after([hidden[1][dy] for dy in range(NY)], met),
        grads,
    )
    sums_a, sums_b = after((sums_a, sums_b), messages)
    near_far = home_z(add(*sums_a), add(*sums_b), 1)
    last = home_x(*after(near_far, acts))
    acts = unpack(place, ids_t, last, 1, 0, width, acts)
    return acts, gate_up, down


def solution(mesh):
    return jax.shard_map(
        on_device,
        mesh=mesh,
        in_specs=(
            P("pipe", None, "expert", None),
            P("pipe", None, "expert", None, None, None),
            P("pipe", None, "expert", None),
            P("pipe", None, "expert", None),
            P("pipe", None, None, "expert"),
            P("pipe", "expert", None),
        ),
        out_specs=(
            P("pipe", None, "expert", None),
            P("pipe", None, None, "expert"),
            P("pipe", "expert", None),
        ),
        check_vma=False,
    )
```

```python
import functools

import jax
import jax.numpy as jnp
from jax import lax
from jax.experimental import pallas as pl
from jax.experimental.pallas import tpu as pltpu
from jax.sharding import PartitionSpec as P

CAP = 20
TOPK = 2
NX = 4
NY = 4
NZ = 2
PAIR = NX * NZ
HALF = NX * CAP
CHUNK = NZ * HALF
MESSAGE = NZ * CAP

SIZES = (192, 256, 192)
DEPTH = 2


bf16 = jnp.bfloat16
f32 = jnp.float32
LIGHT = pl.CostEstimate(flops=1, bytes_accessed=1, transcendentals=0)


def to_y(value, step):
    return lax.ppermute(
        value,
        "expert",
        [(e, e // NY * NY + (e + step) % NY) for e in range(PAIR * NY)],
    )


def to_x(value, step):
    def there(e):
        z, x, y = e // (NX * NY), e // NY % NX, e % NY
        return (z * NX + (x + step) % NX) * NY + y

    return lax.ppermute(value, "expert", [(e, there(e)) for e in range(PAIR * NY)])


def to_z(value):
    return lax.ppermute(
        value, "expert", [(e, e ^ (NX * NY)) for e in range(PAIR * NY)]
    )


def to_mirror(value, flip_z):
    count = PAIR * NY
    half = lax.axis_size("pipe") // 2
    flip = NX * NY if flip_z else 0
    pairs = [
        (p * count + e, (p ^ half) * count + (e ^ flip))
        for p in range(lax.axis_size("pipe"))
        for e in range(count)
    ]
    return lax.ppermute(value, ("pipe", "expert"), pairs)


def after(value, *others):
    return lax.optimization_barrier((value, others))[0]


def to_column(row):
    n = row.shape[1]
    first = lax.broadcasted_iota(jnp.int32, (n, n), 0)
    second = lax.broadcasted_iota(jnp.int32, (n, n), 1)
    return jnp.sum(jnp.where(first == second, row, jnp.zeros_like(row)), axis=1, keepdims=True)


def slot_rows(ids, z, x, along):
    slots = []
    tokens = ids[0].shape[along]
    wide = (PAIR, tokens) if along == 1 else (tokens, PAIR)
    expert = lax.broadcasted_iota(jnp.int32, wide, 1 - along)
    named = [expert == one for one in ids]
    both = (named[0] | named[1]).astype(f32).astype(bf16)
    first = lax.broadcasted_iota(jnp.int32, (tokens, tokens), 0)
    second = lax.broadcasted_iota(jnp.int32, (tokens, tokens), 1)
    if along == 1:
        earlier = jnp.dot(both, (first < second).astype(f32).astype(bf16), preferred_element_type=f32)
    else:
        earlier = jnp.dot((second < first).astype(f32).astype(bf16), both, preferred_element_type=f32)
    for one, mask in zip(ids, named):
        slot = jnp.sum(jnp.where(mask, earlier, 0.0), axis=1 - along, keepdims=True)
        dx = (one - x) & (NX - 1)
        dz = (one // NX) ^ z
        slots.append(dx * MESSAGE + dz * CAP + slot.astype(jnp.int32))
    return slots


def pack_kernel(place, ids_ref, weights_ref, grad_ref, *outs):
    z, x = place[0], place[1]
    for k in range(2):
        ids = [ids_ref[k, r : r + 1, :] for r in range(TOPK)]
        rows = slot_rows(ids, z, x, 1)
        grad = grad_ref[0, k].astype(f32)
        row = lax.broadcasted_iota(jnp.int32, (PAIR * CAP, grad.shape[0]), 0)
        packed = None
        for r in range(TOPK):
            weighted = (to_column(weights_ref[k, r : r + 1, :]) * grad).astype(bf16)
            table = (row == rows[r]).astype(f32).astype(bf16)
            term = jnp.dot(table, weighted, preferred_element_type=f32)
            packed = term if packed is None else packed + term
        for dx in range(NX):
            piece = packed[dx * MESSAGE : (dx + 1) * MESSAGE].astype(bf16)
            outs[dx][k * MESSAGE : (k + 1) * MESSAGE, :] = piece


def pack(place, ids_t, weights_t, grad):
    tokens, width = grad.shape[2:]
    block = width // 2
    return pl.pallas_call(
        pack_kernel,
        grid_spec=pltpu.PrefetchScalarGridSpec(
            num_scalar_prefetch=1,
            grid=(width // block,),
            in_specs=[
                pl.BlockSpec((2, TOPK, tokens), lambda i, s: (0, 0, 0)),
                pl.BlockSpec((2, TOPK, tokens), lambda i, s: (0, 0, 0)),
                pl.BlockSpec((1, 2, tokens, block), lambda i, s: (0, 0, 0, i)),
            ],
            out_specs=[pl.BlockSpec((2 * MESSAGE, block), lambda i, s: (0, i))] * NX,
        ),
        out_shape=[jax.ShapeDtypeStruct((2 * MESSAGE, width), bf16)] * NX,
        compiler_params=pltpu.CompilerParams(vmem_limit_bytes=32 << 20),
        cost_estimate=LIGHT,
        name="pack",
    )(place, ids_t, weights_t, grad)


def unpack_kernel(place, ids_ref, *refs):
    z, x = place[0], place[1]
    parts, out = refs[:NX], refs[-1]
    ids = [to_column(ids_ref[0, r : r + 1, :].astype(f32)).astype(jnp.int32) for r in range(TOPK)]
    rows = slot_rows(ids, z, x, 0)
    tokens = ids[0].shape[0]
    total = None
    for dx in range(NX):
        column = lax.broadcasted_iota(jnp.int32, (tokens, MESSAGE), 1) + dx * MESSAGE
        table = ((column == rows[0]) | (column == rows[1])).astype(f32).astype(bf16)
        term = jnp.dot(table, parts[dx][...], preferred_element_type=f32)
        total = term if total is None else total + term
    out[0, 0] = total.astype(bf16)


def unpack(place, ids_t, parts, micro, first, width, before):
    tokens, block = ids_t.shape[2], parts[0].shape[1]
    in_specs = [pl.BlockSpec((1, TOPK, tokens), lambda i, s: (micro, 0, 0))]
    in_specs += [pl.BlockSpec((MESSAGE, block), lambda i, s: (0, 0))] * NX
    operands = [place, ids_t, *parts]
    aliases = {}
    if before is not None:
        in_specs.append(pl.BlockSpec(memory_space=pl.ANY))
        operands.append(before)
        aliases = {len(operands) - 1: 0}
    return pl.pallas_call(
        unpack_kernel,
        grid_spec=pltpu.PrefetchScalarGridSpec(
            num_scalar_prefetch=1,
            grid=(1,),
            in_specs=in_specs,
            out_specs=pl.BlockSpec((1, 1, tokens, block), lambda i, s: (0, micro, 0, first)),
        ),
        out_shape=jax.ShapeDtypeStruct((1, 2, tokens, width), bf16),
        input_output_aliases=aliases,
        compiler_params=pltpu.CompilerParams(vmem_limit_bytes=32 << 20),
        cost_estimate=LIGHT,
        name="unpack",
    )(*operands)


def kept_row(place, row):
    half = sum((row >= k * HALF).astype(jnp.int32) for k in range(1, NY * NZ))
    left = row - half * HALF
    dx = sum((left >= k * CAP).astype(jnp.int32) for k in range(1, NX))
    slot = left - dx * CAP
    dy, dz = half // NZ, half & (NZ - 1)
    source = ((place[0] ^ dz) * NX + ((place[1] - dx) & (NX - 1))) * NY
    source = source + ((place[2] - dy) & (NY - 1))
    return slot * (PAIR * NY) + source


def ahead_kernel(x_ref, w_ref, out):
    x = x_ref[...]
    units = w_ref.shape[3]
    for i in range(2):
        kept = jnp.dot(x, w_ref[0, i], preferred_element_type=f32)
        high = kept.astype(bf16)
        out[:, 2 * i * units : (2 * i + 1) * units] = high
        out[:, (2 * i + 1) * units : (2 * i + 2) * units] = (kept - high.astype(f32)).astype(bf16)


def ahead(piece, count, w_gate_up):
    width, units = w_gate_up.shape[2:]
    return pl.pallas_call(
        ahead_kernel,
        grid=(1,),
        in_specs=[
            pl.BlockSpec((count, width), lambda i: (0, 0)),
            pl.BlockSpec((1, 2, width, units), lambda i: (0, 0, 0, 0)),
        ],
        out_specs=pl.BlockSpec((count, 4 * units), lambda i: (0, 0)),
        out_shape=jax.ShapeDtypeStruct((count, 4 * units), bf16),
        compiler_params=pltpu.CompilerParams(vmem_limit_bytes=32 << 20),
        cost_estimate=LIGHT,
        name="ahead",
    )(piece, w_gate_up)


def across(a, b):
    return lax.dot_general(a, b, (((1,), (1,)), ((), ())), preferred_element_type=f32)


def part_kernel(pieces, dy, place, *refs):
    gs, refs = refs[:pieces], refs[pieces:]
    ya_ref, yb_ref, w_ref, d_ref, *outs = refs
    h_ref = outs[-1]
    units = d_ref.shape[1]
    wanted = kept_row(place, lax.broadcasted_iota(jnp.int32, (CHUNK, 1), 0) + dy * CHUNK)
    column = lax.broadcasted_iota(jnp.int32, (CHUNK, NY * CHUNK), 1)
    table = (column == wanted).astype(f32).astype(bf16)
    kept = jnp.concatenate([ref[...] for ref in gs], axis=0)
    kept = jnp.dot(table, kept, preferred_element_type=f32)
    gate = kept[:, :units] + kept[:, units : 2 * units]
    up = kept[:, 2 * units : 3 * units] + kept[:, 3 * units :]
    y = jnp.concatenate([ya_ref[...], yb_ref[...]], axis=0)
    back = across(y, d_ref[0])
    sigmoid = jax.nn.sigmoid(gate)
    activated = gate * sigmoid
    back_gate = (back * up * sigmoid * (1.0 + gate * (1.0 - sigmoid))).astype(bf16)
    back_up = (back * activated).astype(bf16)
    h_ref[:, 0:units] = back_gate
    h_ref[:, units : 2 * units] = back_up
    h_ref[:, 2 * units : 3 * units] = (activated * up).astype(bf16)
    part = across(back_gate, w_ref[0, 0]) + across(back_up, w_ref[0, 1])
    cuts = len(outs) // NZ
    block = part.shape[1] // cuts
    for dz in range(NZ):
        for cut in range(cuts):
            piece = part[dz * HALF : (dz + 1) * HALF, cut * block : (cut + 1) * block]
            outs[cut * NZ + dz][...] = piece.astype(bf16)


def part_pass(place, gates, dy, ya, yb, w_gate_up, w_down, cuts):
    width = ya.shape[1]
    units = w_down.shape[1]
    cut = pl.BlockSpec((HALF, width // cuts), lambda i, s: (0, 0))
    return pl.pallas_call(
        functools.partial(part_kernel, len(gates), dy),
        grid_spec=pltpu.PrefetchScalarGridSpec(
            num_scalar_prefetch=1,
            grid=(1,),
            in_specs=[pl.BlockSpec(g.shape, lambda i, s: (0, 0)) for g in gates]
            + [
                pl.BlockSpec((HALF, width), lambda i, s: (0, 0)),
                pl.BlockSpec((HALF, width), lambda i, s: (0, 0)),
                pl.BlockSpec((1, 2, width, units), lambda i, s: (0, 0, 0, 0)),
                pl.BlockSpec((1, units, width), lambda i, s: (0, 0, 0)),
            ],
            out_specs=[cut] * (NZ * cuts) + [pl.BlockSpec((CHUNK, 3 * units), lambda i, s: (0, 0))],
        ),
        out_shape=[jax.ShapeDtypeStruct((HALF, width // cuts), bf16)] * (NZ * cuts)
        + [jax.ShapeDtypeStruct((CHUNK, 3 * units), bf16)],
        compiler_params=pltpu.CompilerParams(vmem_limit_bytes=32 << 20),
        cost_estimate=LIGHT,
        name="part",
    )(place, *gates, ya, yb, w_gate_up, w_down)


def share_kernel(pieces, more, place, *refs):
    xs, refs = refs[:pieces], refs[pieces:]
    ys, hs, refs = refs[: NZ * NY], refs[NZ * NY : NZ * NY + NY], refs[NZ * NY + NY :]
    before, refs = refs[:more], refs[more:]
    gate_up_ref, down_ref, moved, hidden = refs
    units = down_ref.shape[1]
    rows = NY * CHUNK

    @pl.when(pl.program_id(0) == 0)
    def _():
        wanted = kept_row(place, lax.broadcasted_iota(jnp.int32, (1, rows), 1))
        row = lax.broadcasted_iota(jnp.int32, (rows, rows), 0)
        table = (row == wanted).astype(f32).astype(bf16)
        h = jnp.concatenate([r[...] for r in hs], axis=0)
        kept = jnp.dot(table, h[:, : 2 * units], preferred_element_type=f32)
        moved[...] = kept.astype(bf16)
        hidden[...] = h[:, 2 * units :]

    x = jnp.concatenate([r[...] for r in xs], axis=0)
    y = jnp.concatenate([r[...] for r in ys], axis=0)

    def over_rows(a, b):
        return lax.dot_general(a, b, (((0,), (0,)), ((), ())), preferred_element_type=f32)

    gate_up = over_rows(x, moved[...])
    share = [gate_up[:, :units], gate_up[:, units:], over_rows(hidden[...], y)]
    if before:
        share[0] = share[0] + before[0][0, 0].astype(f32)
        share[1] = share[1] + before[0][0, 1].astype(f32)
        share[2] = share[2] + before[1][0].astype(f32)
    gate_up_ref[0, 0] = share[0].astype(bf16)
    gate_up_ref[0, 1] = share[1].astype(bf16)
    down_ref[0] = share[2].astype(bf16)


def shares(place, xs, sizes, ys, hs, before):
    width = ys[0].shape[1]
    units = hs[0].shape[1] // 3
    block = 512 if width % 512 == 0 else 256
    by_column = [pl.BlockSpec((size, block), lambda i, s: (0, i)) for size in sizes]
    by_column += [pl.BlockSpec((HALF, block), lambda i, s: (0, i))] * (NZ * NY)
    whole = [pl.BlockSpec((CHUNK, 3 * units), lambda i, s: (0, 0))] * NY
    outs = [
        pl.BlockSpec((1, 2, block, units), lambda i, s: (0, 0, i, 0)),
        pl.BlockSpec((1, units, block), lambda i, s: (0, 0, i)),
    ]
    return pl.pallas_call(
        functools.partial(share_kernel, len(xs), len(before)),
        grid_spec=pltpu.PrefetchScalarGridSpec(
            num_scalar_prefetch=1,
            grid=(width // block,),
            in_specs=by_column + whole + outs[: len(before)],
            out_specs=outs,
            scratch_shapes=[
                pltpu.VMEM((NY * CHUNK, 2 * units), bf16),
                pltpu.VMEM((NY * CHUNK, units), bf16),
            ],
        ),
        out_shape=[
            jax.ShapeDtypeStruct((1, 2, width, units), bf16),
            jax.ShapeDtypeStruct((1, units, width), bf16),
        ],
        compiler_params=pltpu.CompilerParams(vmem_limit_bytes=32 << 20),
        cost_estimate=LIGHT,
        name="shares",
    )(place, *xs, *ys, *hs, *before)


def add(*terms):
    total = terms[0].astype(f32)
    for term in terms[1:]:
        total = total + term.astype(f32)
    return total.astype(bf16)


def over_x(blocks):
    return [blocks[0]] + [to_x(blocks[dx], dx) for dx in range(1, NX)]


def over_z(messages, micro):
    at = micro * MESSAGE
    near = jnp.concatenate([m[at : at + CAP] for m in messages], axis=0)
    far = jnp.concatenate([m[at + CAP : at + MESSAGE] for m in messages], axis=0)
    if micro == 0:
        return near, to_z(far)
    return to_mirror(near, False), to_mirror(far, True)


class Ring:
    def __init__(self):
        self.done = {1: [], -1: []}

    def send(self, value, step, *events):
        before = len(self.done[step]) - DEPTH
        if before >= 0:
            events += tuple(done[before] for done in self.done.values() if len(done) > before)
        self.done[step].append(to_y(after(value, *events) if events else value, step))
        return self.done[step][-1]


def home_z(a, b, micro):
    if micro == 0:
        return a, to_z(b)
    return to_mirror(a, False), to_mirror(b, True)


def home_x(near, far):
    messages = []
    for dx in range(NX):
        rows = slice(dx * CAP, (dx + 1) * CAP)
        message = jnp.concatenate([near[rows], far[rows]], axis=0)
        messages.append(to_x(message, -dx) if dx else message)
    return messages


def on_device(grad_out, x_slots, expert_ids, route_weights, w_gate_up, w_down):
    e = lax.axis_index("expert")
    width = grad_out.shape[-1]
    place = jnp.stack([e // (NX * NY), e // NY % NX, e % NY]).astype(jnp.int32)
    ids_t = jnp.swapaxes(expert_ids[0], 1, 2)
    weights_t = jnp.swapaxes(route_weights[0], 1, 2)
    rows = jnp.swapaxes(x_slots, 3, 4).reshape(-1, width)
    every = NY * CHUNK
    order = (2, 1, 3, 0)
    starts = [every + sum(SIZES[:i]) for i in range(len(SIZES))]
    moved = []

    def move(*events):
        at, size = starts[len(moved)], SIZES[len(moved)]
        value = rows[at : at + size]
        moved.append(to_mirror(after(value, *events) if events else value, False))

    ring = Ring()

    messages = over_x(pack(place, ids_t, weights_t, grad_out))
    gates = ahead(rows, every, w_gate_up)
    move()
    messages = after(messages, gates, moved[0])
    a, b = over_z(messages, 0)
    near_far = over_z(messages, 1)
    up_a, down_a = ring.send(a, 1), ring.send(a, -1)
    cut = HALF // 2
    over_a = [ring.send(up_a[:cut], 1), ring.send(down_a[cut:], -1)]
    b = after(b, up_a, down_a, over_a)
    up_b, down_b = ring.send(b, 1), ring.send(b, -1)
    over_b = [ring.send(up_b[:cut], 1, *near_far), ring.send(down_b[cut:], -1, *near_far)]
    twice_a, twice_b = jnp.concatenate(over_a, axis=0), jnp.concatenate(over_b, axis=0)
    slots = [[(a, b), (up_a, up_b), (twice_a, twice_b), (down_a, down_b)]]
    move(near_far, moved[0])
    a, b = near_far
    up_a, down_a = ring.send(a, 1), ring.send(a, -1)
    up_b, down_b = ring.send(b, 1), ring.send(b, -1)
    hidden = [{}, {}]

    def compute(k, gates):
        parts = [None] * NY
        for dy in order:
            *parts[dy], hidden[k][dy] = part_pass(
                place, gates, dy, *slots[k][dy], w_gate_up, w_down, 1
            )
        return parts

    def sum_up(parts, *between):
        met = ring.send(parts[2][1], 1), ring.send(parts[2][0], -1)
        b1 = ring.send(parts[1][1], -1)
        a3 = ring.send(parts[3][0], 1)
        a1 = ring.send(add(parts[1][0], met[1]), -1, *between)
        b3 = ring.send(add(parts[3][1], met[0]), 1, *between)
        return met, (parts[0][0], a1, a3), (parts[0][1], b1, b3)

    twice_a, twice_b = ring.send(up_a, 1, moved[1]), ring.send(down_b, -1, moved[1])
    slots.append([(a, b), (up_a, up_b), (twice_a, twice_b), (down_a, down_b)])
    move(moved[1])
    parts = compute(0, [gates])
    met, sums_a, sums_b = sum_up(parts, moved[2])
    back = home_z(add(*sums_a), add(*sums_b), 0)
    messages = home_x(*back)
    acts = unpack(place, ids_t, messages, 0, 0, width, None)
    grads = shares(
        place,
        [rows],
        [every],
        [half for dy in range(NY) for half in slots[0][dy]],
        after([hidden[0][dy] for dy in range(NY)], met),
        [],
    )

    *early, last = moved
    gates = [ahead(piece, size, w_gate_up) for piece, size in zip(early, SIZES)]
    gates.append(ahead(after(last, met, gates, grads), SIZES[-1], w_gate_up))
    parts = compute(1, gates)
    met, sums_a, sums_b = sum_up(parts, *back)
    gate_up, down = shares(
        place,
        moved,
        SIZES,
        [half for dy in range(NY) for half in slots[1][dy]],
        after([hidden[1][dy] for dy in range(NY)], met),
        grads,
    )
    sums_a, sums_b = after((sums_a, sums_b), messages)
    near_far = home_z(add(*sums_a), add(*sums_b), 1)
    last = home_x(*after(near_far, acts))
    acts = unpack(place, ids_t, last, 1, 0, width, acts)
    return acts, gate_up, down


def solution(mesh):
    return jax.shard_map(
        on_device,
        mesh=mesh,
        in_specs=(
            P("pipe", None, "expert", None),
            P("pipe", None, "expert", None, None, None),
            P("pipe", None, "expert", None),
            P("pipe", None, "expert", None),
            P("pipe", None, None, "expert"),
            P("pipe", "expert", None),
        ),
        out_specs=(
            P("pipe", None, "expert", None),
            P("pipe", None, None, "expert"),
            P("pipe", "expert", None),
        ),
        check_vma=False,
    )
```
